512 devices in a mesh: dom: 128 (over z, y, core), feat: 4 (over x).
Axes of the slice: x: 4, y: 4, z: 16, core: 2. Of those that a mesh axis runs over, the one named last changes fastest.
Arguments:
- features: bfloat16 [131072, 256], P('dom', 'feat'), may hold values from -6 to 6
- keep_cols: int32 [128], P('feat'), may hold values from 0 to 63, as said below
- send_rows: int32 [128, 128, 128], P('dom'), may hold values from 0 to 1024, as said below
- tile_cols: int32 [4096], P('dom'), may hold values from 0 to 135
- tile_vals: bfloat16 [4096, 128, 128], P('dom'), may hold values from -0.25 to 0.25
- weight: bfloat16 [128, 256], P('feat'), may hold values from -0.5 to 0.5
- bias: float32 [256], P('feat'), may hold values from -3 to 3
- grad_out: bfloat16 [131072, 256], P('dom', 'feat'), may hold values from -0.015625 to 0.015625
Outputs:
- out: bfloat16 [131072, 256], P('dom', 'feat')
- grad_weight: float32 [128, 256], P(None, 'feat')
- grad_bias: float32 [256], P('feat')
The draws below stay inside these ranges and needn't reach their ends.
Inputs may be any that keep to these rules, and one draw needn't show every extreme that they name: `keep_cols`: each block of 128 / 4 entries is increasing, holds distinct values and includes 0 and 256 / 4 - 1. send_rows[p, q] lists rows of partition p that partition q reads; the used slots come first and are distinct rows, the rest are 1024; some lists are full and some have one used slot.
All inputs are finite; a program needn't handle non-finite values.
Results may differ from the reference program's by a relative error of at most 0.001.
Values may be sent and summed in bfloat16 or wider, within the bound.
No kernel may reach another device: no remote copies, remote signals or barrier semaphores. Data moves between devices by JAX's collectives and lax.ppermute only.
A program may use at most 64 MiB of HBM per device.

```python
import jax
import jax.numpy as jnp
from jax import lax

F_IN = 256
KEEP = 128
HID = 256
ROWS = 1024
BLK = 128
TPR = 4
RTILES = 8
NTILE = 32
EXT_TILES = 136
NODES = 131072
N_DOM = 128
N_FEAT = 4


def draw_keep_cols(key, part):
    key = jax.random.fold_in(key, 1)
    cols_local = F_IN // N_FEAT
    per_block = KEEP // N_FEAT
    keys = jax.random.split(key, N_FEAT)

    def pick_block(block_key):
        inner = jax.random.permutation(block_key, cols_local - 2)[:per_block - 2].astype(jnp.int32) + 1
        whole = jnp.concatenate([jnp.zeros((1,), jnp.int32), inner, jnp.full((1,), cols_local - 1, jnp.int32)])
        return jnp.sort(whole)
    return jax.vmap(pick_block)(keys).reshape(KEEP).astype(jnp.int32)


def draw_send_rows(key, part):
    key = jax.random.fold_in(key, 2)
    first_key, second_key, list_key = jax.random.split(key, 3)
    first = jax.random.randint(first_key, (N_DOM, N_DOM), 0, BLK)
    second = jax.random.randint(second_key, (N_DOM, N_DOM), 0, BLK)
    count = jnp.minimum(first, second) + 1
    sender = jnp.arange(N_DOM, dtype=jnp.int32)[:, None]
    receiver = jnp.arange(N_DOM, dtype=jnp.int32)[None, :]
    count = jnp.where(receiver == (sender + 1) % N_DOM, BLK, count)
    count = jnp.where(receiver == sender, 1, count)

    def make_lists(row_key):
        scores = jax.random.randint(row_key, (N_DOM, ROWS), 0, 1 << 18) * ROWS + jnp.arange(ROWS, dtype=jnp.int32)[None, :]
        order = jnp.argsort(scores, axis=1, stable=True)[:, :BLK]
        return order.astype(jnp.int32)
    lists = lax.map(make_lists, jax.random.split(list_key, N_DOM))
    slot = jnp.arange(BLK, dtype=jnp.int32)
    return jnp.where(slot[None, None, :] < count[:, :, None], lists, ROWS).astype(jnp.int32)


def place_ends(array, stream_key, least, top_value):
    dims = array.shape
    index_at = [jax.random.randint(jax.random.fold_in(stream_key, axis), (), 0, dims[axis]) for axis in range(len(dims))]
    array = array.at[tuple(index_at)].set(least)
    longest = dims.index(max(dims))
    index_at[longest] = (index_at[longest] + 1) % dims[longest]
    return array.at[tuple(index_at)].set(top_value)


def levels(rng, dims, cuts, smallest, top_value):
    def one(position, blocks):
        heights = jax.random.uniform(jax.random.fold_in(jax.random.fold_in(rng, 6), position), (blocks,), jnp.float32, smallest / len(cuts), top_value / len(cuts))
        return jnp.repeat(jnp.exp(heights), dims[position] // blocks).reshape((-1,) + (1,) * (len(dims) - position - 1))

    factor_of = one(*cuts[0])
    for cut in cuts[1:]:
        factor_of = factor_of * one(*cut)
    return factor_of


def bell_draw(stream_key, shape, spread, limit, cuts=(), kind=jnp.bfloat16):
    result = jax.random.normal(stream_key, shape, jnp.float32) * spread
    if len(cuts) > 0:
        result = levels(stream_key, shape, cuts, -0.22, 0.18) * result
    return jnp.clip(result, min=-limit, max=limit).astype(kind)


def setup_inputs(seed: int = 0) -> dict:
    splits = jax.random.split(jax.random.key(seed), 9)
    return {
        "features": bell_draw(splits[0], (NODES, F_IN), 1.0, 6.0, ((0, 128), (1, 4))),
        "keep_cols": draw_keep_cols(jax.random.fold_in(splits[8], 71), 0),
        "send_rows": draw_send_rows(jax.random.fold_in(splits[8], 71), 0),
        "tile_cols": place_ends(jax.random.randint(splits[3], (N_DOM * NTILE,), 0, EXT_TILES), jax.random.fold_in(splits[3], 1), 0, EXT_TILES - 1).astype(jnp.int32),
        "tile_vals": bell_draw(splits[4], (N_DOM * NTILE, BLK, BLK), (TPR * BLK) ** -0.5, 0.25, ((0, 128),)),
        "weight": bell_draw(splits[5], (KEEP, HID), KEEP ** -0.5, 0.5, ((0, 4),)),
        "bias": bell_draw(splits[6], (HID,), 0.5, 3.0, ((0, 4),), jnp.float32),
        "grad_out": bell_draw(splits[7], (NODES, HID), NODES ** -0.5, 0.015625, ((0, 128), (1, 4))),
    }


def activation(value):
    return jax.nn.gelu(value, approximate=True)

def reference(features, keep_cols, send_rows, tile_cols, tile_vals, weight, bias, grad_out):
    per_block = KEEP // N_FEAT
    cols_local = F_IN // N_FEAT
    global_cols = jnp.arange(KEEP, dtype=jnp.int32) // per_block * cols_local + keep_cols
    kept = jnp.take(features, global_cols, axis=1)
    kept_dev = kept.reshape(N_DOM, ROWS, KEEP)
    padded = jnp.concatenate([kept_dev, jnp.zeros((N_DOM, 1, KEEP), kept.dtype)], axis=1)
    senders = jnp.arange(N_DOM, dtype=jnp.int32)[:, None]

    def one_part(part_index):
        lists = send_rows[:, part_index, :]
        halo_rows = padded[senders, lists]
        extended = jnp.concatenate([kept_dev[part_index], halo_rows.reshape(N_DOM * BLK, KEEP)], axis=0)
        extended = extended.reshape(EXT_TILES, BLK, KEEP).astype(jnp.float32)
        columns = lax.dynamic_slice_in_dim(tile_cols, part_index * NTILE, NTILE)
        values = lax.dynamic_slice_in_dim(tile_vals, part_index * NTILE, NTILE).astype(jnp.float32)
        picked = jnp.take(extended, columns, axis=0)
        product = jnp.einsum('tij,tjc->tic', values, picked, precision=lax.Precision.HIGHEST)
        return product.reshape(RTILES, TPR, BLK, KEEP).sum(axis=1).reshape(ROWS, KEEP)
    aggregated = lax.map(one_part, jnp.arange(N_DOM, dtype=jnp.int32)).reshape(NODES, KEEP)
    pre = jnp.dot(aggregated, weight.astype(jnp.float32), precision=lax.Precision.HIGHEST) + bias
    out, pull = jax.vjp(activation, pre)
    grad_pre, = pull(grad_out.astype(jnp.float32))
    grad_weight = jnp.dot(aggregated.T, grad_pre, precision=lax.Precision.HIGHEST)
    grad_bias = lax.optimization_barrier(jnp.sum(grad_pre, axis=0))
    return (out.astype(jnp.bfloat16), grad_weight, grad_bias)
```

```python
import functools
import math

import jax
import jax.numpy as jnp
from jax import lax
from jax.experimental import pallas as pl
from jax.experimental.pallas import tpu as pltpu
from jax.sharding import Mesh, PartitionSpec as P

DOM = ("z", "y", "core")
PLANE = ("y", "core")
NT = (((1,), (1,)), ((), ()))
LOW = 256
F32 = jnp.float32
BF16 = jnp.bfloat16


def pick_kernel(keep_ref, features_ref, lists_ref, out_ref, kept_ref, table):
    kept = kept_ref.shape[1]
    block = kept_ref.shape[2]
    highs = features_ref.shape[0] // LOW

    @pl.when(pl.program_id(0) == 0)
    def _():
        lane = lax.broadcasted_iota(jnp.int32, (kept, features_ref.shape[1]), 1)
        select = jnp.where(lane == keep_ref[...], 1.0, 0.0).astype(BF16)
        columns = lax.dot_general(select, features_ref[...], NT, preferred_element_type=F32)
        columns = columns.astype(BF16)
        for tile in range(kept_ref.shape[0]):
            kept_ref[tile] = columns[:, tile * block : (tile + 1) * block]
        for high in range(highs):
            table[high * kept : (high + 1) * kept, :] = columns[:, high * LOW : (high + 1) * LOW]

    for pair in range(lists_ref.shape[0] // 2):
        rows = jnp.concatenate(
            [lists_ref[2 * pair : 2 * pair + 1, :], lists_ref[2 * pair + 1 : 2 * pair + 2, :]], axis=1
        )
        low = rows & (LOW - 1)
        high = rows // LOW
        sub = lax.broadcasted_iota(jnp.int32, (LOW, 2 * block), 0)
        onehot = jnp.where(sub == low, 1.0, 0.0).astype(BF16)
        found = jnp.dot(table[...], onehot, preferred_element_type=F32)
        total = jnp.zeros((kept, 2 * block), F32)
        for step in range(highs):
            total = jnp.where(high == step, found[step * kept : (step + 1) * kept], total)
        total = total.astype(BF16)
        out_ref[2 * pair] = total[:, :block]
        out_ref[2 * pair + 1] = total[:, block:]


def pick(keep_cols, features, lists):
    peers, block = lists.shape
    rows = features.shape[0]
    kept = keep_cols.shape[0]
    step = 16
    return pl.pallas_call(
        pick_kernel,
        grid=(peers // step,),
        in_specs=[
            pl.BlockSpec((kept, 1), lambda i: (0, 0)),
            pl.BlockSpec(features.shape, lambda i: (0, 0)),
            pl.BlockSpec((step, block), lambda i: (i, 0)),
        ],
        out_specs=[
            pl.BlockSpec((step, kept, block), lambda i: (i, 0, 0)),
            pl.BlockSpec((rows // block, kept, block), lambda i: (0, 0, 0)),
        ],
        out_shape=[
            jax.ShapeDtypeStruct((peers, kept, block), BF16),
            jax.ShapeDtypeStruct((rows // block, kept, block), BF16),
        ],
        scratch_shapes=[pltpu.VMEM((rows // LOW * kept, LOW), BF16)],
        compiler_params=pltpu.CompilerParams(vmem_limit_bytes=24 << 20),
        name="pick_rows",
    )(keep_cols[:, None], features, lists)


def aggregate_kernel(tiles_row, cols_ref, own_ref, incoming_ref, vals_ref, out_ref):
    own = own_ref.shape[0]
    block = own_ref.shape[2]
    for tile in range(vals_ref.shape[0] // tiles_row):
        values, picked = [], []
        for term in range(tiles_row):
            at = tile * tiles_row + term
            column = cols_ref[at]
            mine = own_ref[jnp.minimum(column, own - 1)]
            theirs = incoming_ref[jnp.maximum(column - own, 0)]
            picked.append(jnp.where(column < own, mine, theirs))
            values.append(vals_ref[at])
        out_ref[:, tile * block : (tile + 1) * block] = lax.dot_general(
            jnp.concatenate(picked, axis=1), jnp.concatenate(values, axis=1), NT, preferred_element_type=F32
        )


def aggregate(tile_cols, own, incoming, tile_vals):
    tiles, kept, block = own.shape
    vmem = pl.BlockSpec(memory_space=pltpu.VMEM)
    return pl.pallas_call(
        functools.partial(aggregate_kernel, tile_cols.shape[0] // tiles),
        in_specs=[pl.BlockSpec(memory_space=pltpu.SMEM), vmem, vmem, vmem],
        out_specs=vmem,
        out_shape=jax.ShapeDtypeStruct((kept, tiles * block), F32),
        compiler_params=pltpu.CompilerParams(vmem_limit_bytes=24 << 20),
        name="aggregate_tiles",
    )(tile_cols, own, incoming, tile_vals)


def layer_kernel(agg_ref, weight_ref, bias_ref, grad_ref, out_ref, terms_ref):
    hidden, nodes = grad_ref.shape
    step = 256
    depth = agg_ref.shape[0]
    slope = math.sqrt(2.0 / math.pi)
    weight = jnp.concatenate([weight_ref[...]] * 3, axis=1)
    grad_weight = jnp.zeros((hidden, depth), F32)
    grad_bias = jnp.zeros((hidden, 1), F32)
    for start in range(0, nodes, step):
        exact = agg_ref[:, start : start + step]
        first = exact.astype(BF16)
        rest = exact - first.astype(F32)
        second = rest.astype(BF16)
        third = (rest - second.astype(F32)).astype(BF16)
        pre = jnp.dot(weight, jnp.concatenate([first, second, third], axis=0), preferred_element_type=F32)
        pre = pre + bias_ref[...]
        square = pre * pre
        bend = jnp.tanh(slope * (pre + 0.044715 * (pre * square)))
        half = 0.5 * (1.0 + bend)
        out_ref[start : start + step, :] = (pre * half).T.astype(BF16)
        inner = slope * (1.0 + 3 * 0.044715 * square)
        pull = half + 0.5 * pre * ((1.0 - bend) * (1.0 + bend)) * inner
        grad_pre = grad_ref[:, start : start + step].astype(F32) * pull
        grad_bias += jnp.sum(grad_pre, axis=1, keepdims=True)
        upper = grad_pre.astype(BF16)
        lower = (grad_pre - upper.astype(F32)).astype(BF16)
        both = lax.dot_general(
            jnp.concatenate([upper, lower], axis=0),
            jnp.concatenate([first, second], axis=0),
            NT,
            preferred_element_type=F32,
        )
        grad_weight += (both[:hidden, depth:] + both[hidden:, :depth]) + both[:hidden, :depth]
    groups = terms_ref.shape[0]
    terms_ref[:, : hidden // groups, :] = grad_weight.reshape(groups, hidden // groups, depth)
    terms_ref[:, hidden // groups :, :] = jnp.broadcast_to(grad_bias, (hidden, depth)).reshape(
        groups, hidden // groups, depth
    )


def layer(aggregated, weight, bias, grad_out, groups):
    depth, nodes = aggregated.shape
    hidden = weight.shape[0]
    vmem = pl.BlockSpec(memory_space=pltpu.VMEM)
    return pl.pallas_call(
        layer_kernel,
        in_specs=[vmem] * 4,
        out_specs=[vmem] * 2,
        out_shape=[
            jax.ShapeDtypeStruct((nodes, hidden), BF16),
            jax.ShapeDtypeStruct((groups, 2 * hidden // groups, depth), F32),
        ],
        compiler_params=pltpu.CompilerParams(vmem_limit_bytes=24 << 20),
        name="layer_and_gradient",
    )(aggregated, weight, bias[:, None], grad_out)


def spread(array, axis):
    size = lax.axis_size(axis)
    return lax.all_to_all(jnp.broadcast_to(array[None], (size,) + array.shape), axis, 0, 0)


def shards(features, keep_cols, send_rows, tile_cols, tile_vals, weight, bias, grad_out):
    feat = lax.axis_size("feat")
    hidden = bias.shape[0]
    kept = keep_cols.shape[0]
    outgoing, own = pick(keep_cols, features, send_rows[0])
    incoming = lax.all_to_all(outgoing, DOM, 0, 0, tiled=True)
    blocks = weight.reshape(kept, feat, hidden).transpose(1, 2, 0)
    blocks = lax.all_to_all(blocks, "feat", 0, 0)
    columns = blocks.transpose(1, 0, 2).reshape(hidden, feat * kept)
    aggregated = aggregate(tile_cols, own, incoming, tile_vals)
    aggregated = spread(aggregated, "feat").reshape(feat * kept, -1)
    groups = lax.axis_size(PLANE)
    out, terms = layer(aggregated, columns, bias, grad_out.T, groups)
    terms = lax.all_to_all(terms, PLANE, 0, 0).sum(axis=0)
    terms = spread(terms, "z").sum(axis=0)
    terms = spread(terms, PLANE)
    rows = hidden // groups
    grad_weight = terms[:, :rows].reshape(hidden, feat * kept).T
    grad_bias = terms[:, rows:, 0].reshape(hidden)
    return out, grad_weight, grad_bias


def solution(mesh):
    devices = mesh.devices.reshape(16, 4, 2, mesh.shape["feat"])
    fine = Mesh(devices, DOM + ("feat",))
    placed = (
        P(DOM, "feat"),
        P("feat"),
        P(DOM, None, None),
        P(DOM),
        P(DOM, None, None),
        P("feat", None),
        P("feat"),
        P(DOM, "feat"),
    )
    return jax.shard_map(
        shards,
        mesh=fine,
        in_specs=placed,
        out_specs=(P(DOM, "feat"), P(None, "feat"), P("feat")),
        check_vma=False,
    )
```

```python
import functools
import math

import jax
import jax.numpy as jnp
from jax import lax
from jax.experimental import pallas as pl
from jax.experimental.pallas import tpu as pltpu
from jax.sharding import Mesh, PartitionSpec as P

DOM = ("z_far", "z_near", "y", "core")
NEAR = ("z_near", "y", "core")
PLANE = ("y", "core")
RING = ("z_far", "z_near")
NT = (((1,), (1,)), ((), ()))
LOW = 256
CODE = 128
F32 = jnp.float32
BF16 = jnp.bfloat16


def keep_kernel(keep_ref, features_ref, lists_ref, out_ref):
    planes, rows, block = out_ref.shape
    kept = keep_ref.shape[0]
    nodes = features_ref.shape[1]
    lists = lists_ref.shape[0] // planes
    lane = lax.broadcasted_iota(jnp.int32, (kept, features_ref.shape[0]), 1)
    select = jnp.where(lane == keep_ref[...], 1.0, 0.0).astype(BF16)
    columns = jnp.dot(select, features_ref[...], preferred_element_type=F32).astype(BF16)
    row = lists_ref[...]
    code = lax.shift_left(CODE + (row & (CODE - 1)), row // CODE)
    code = (code.astype(F32) * (1.0 / CODE)).astype(BF16)
    for plane in range(planes):
        for tile in range(nodes // block):
            out_ref[plane, tile * kept : (tile + 1) * kept, :] = columns[:, tile * block : (tile + 1) * block]
        out_ref[plane, rows - lists :, :] = code[plane * lists : (plane + 1) * lists]


def keep(keep_cols, features, lists, planes):
    peers, block = lists.shape
    nodes = features.shape[1]
    kept = keep_cols.shape[0]
    rows = nodes // block * kept + peers // planes
    vmem = pl.BlockSpec(memory_space=pltpu.VMEM)
    return pl.pallas_call(
        keep_kernel,
        in_specs=[vmem] * 3,
        out_specs=vmem,
        out_shape=jax.ShapeDtypeStruct((planes, rows, block), BF16),
        compiler_params=pltpu.CompilerParams(vmem_limit_bytes=24 << 20),
        name="keep_columns",
    )(keep_cols[:, None], features, lists)


def pick_kernel(held_ref, out_ref):
    lists, _, kept, block = out_ref.shape
    tiles = (held_ref.shape[1] - lists) // kept
    span = LOW // block
    highs = tiles // span
    table = jnp.concatenate(
        [
            jnp.concatenate([held_ref[0, t * kept : (t + 1) * kept, :] for t in range(h * span, (h + 1) * span)], axis=1)
            for h in range(highs)
        ],
        axis=0,
    )
    code = (held_ref[0, tiles * kept :, :].astype(F32) * CODE).astype(jnp.int32)
    shift = jnp.zeros((lists, block), jnp.int32)
    for step in range(1, tiles + 1):
        shift += jnp.where(code >= CODE << step, 1, 0)
    row = shift * CODE + (lax.shift_right_logical(code, shift) - CODE)
    sub = lax.broadcasted_iota(jnp.int32, (LOW, 2 * block), 0)
    for pair in range(lists // 2):
        rows = jnp.concatenate([row[2 * pair : 2 * pair + 1, :], row[2 * pair + 1 : 2 * pair + 2, :]], axis=1)
        low = rows & (LOW - 1)
        high = rows // LOW
        onehot = jnp.where(sub == low, 1.0, 0.0).astype(BF16)
        found = jnp.dot(table, onehot, preferred_element_type=F32)
        total = jnp.zeros((kept, 2 * block), F32)
        for step in range(highs):
            total = jnp.where(high == step, found[step * kept : (step + 1) * kept], total)
        total = total.astype(BF16)
        out_ref[2 * pair, 0] = total[:, :block]
        out_ref[2 * pair + 1, 0] = total[:, block:]


def pick(held, lists, kept):
    planes, rows, block = held.shape
    return pl.pallas_call(
        pick_kernel,
        grid=(planes,),
        in_specs=[pl.BlockSpec((1, rows, block), lambda i: (i, 0, 0))],
        out_specs=pl.BlockSpec((lists, 1, kept, block), lambda i: (0, i, 0, 0)),
        out_shape=jax.ShapeDtypeStruct((lists, planes, kept, block), BF16),
        compiler_params=pltpu.CompilerParams(vmem_limit_bytes=24 << 20),
        name="pick_rows",
    )(held)


def aggregate_kernel(tiles_row, cols_ref, own_ref, incoming_ref, vals_ref, out_ref):
    kept, block = incoming_ref.shape[2:]
    own = vals_ref.shape[0] // tiles_row
    near = incoming_ref.shape[0]
    for tile in range(vals_ref.shape[0] // tiles_row):
        values, picked = [], []
        for term in range(tiles_row):
            at = tile * tiles_row + term
            column = cols_ref[at]
            mine = own_ref[pl.ds(pl.multiple_of(jnp.minimum(column, own - 1) * kept, kept), kept), :]
            sender = jnp.maximum(column - own, 0)
            theirs = incoming_ref[sender % near, sender // near]
            picked.append(jnp.where(column < own, mine, theirs))
            values.append(vals_ref[at])
        total = lax.dot_general(
            jnp.concatenate(picked, axis=1), jnp.concatenate(values, axis=1), NT, preferred_element_type=F32
        )
        for copy in range(out_ref.shape[0]):
            out_ref[copy, :, tile * block : (tile + 1) * block] = total


def aggregate(tile_cols, own, incoming, tile_vals, copies):
    kept, block = incoming.shape[2:]
    tiles = own.shape[0] // kept
    vmem = pl.BlockSpec(memory_space=pltpu.VMEM)
    return pl.pallas_call(
        functools.partial(aggregate_kernel, tile_cols.shape[0] // tiles),
        in_specs=[pl.BlockSpec(memory_space=pltpu.SMEM), vmem, vmem, vmem],
        out_specs=vmem,
        out_shape=jax.ShapeDtypeStruct((copies, kept, tiles * block), F32),
        compiler_params=pltpu.CompilerParams(vmem_limit_bytes=24 << 20),
        name="aggregate_tiles",
    )(tile_cols, own, incoming, tile_vals)


def layer_kernel(agg_ref, weight_ref, bias_ref, grad_ref, out_ref, terms_ref):
    hidden, nodes = grad_ref.shape
    step = 256
    depth = agg_ref.shape[0]
    slope = math.sqrt(2.0 / math.pi)
    weight = jnp.concatenate([weight_ref[...]] * 3, axis=1)
    grad_weight = jnp.zeros((hidden, depth), F32)
    grad_bias = jnp.zeros((hidden, 1), F32)
    for start in range(0, nodes, step):
        exact = agg_ref[:, start : start + step]
        first = exact.astype(BF16)
        rest = exact - first.astype(F32)
        second = rest.astype(BF16)
        third = (rest - second.astype(F32)).astype(BF16)
        pre = jnp.dot(weight, jnp.concatenate([first, second, third], axis=0), preferred_element_type=F32)
        pre = pre + bias_ref[...]
        square = pre * pre
        bend = jnp.tanh(slope * (pre + 0.044715 * (pre * square)))
        half = 0.5 * (1.0 + bend)
        out_ref[:, start : start + step] = (pre * half).astype(BF16)
        inner = slope * (1.0 + 3 * 0.044715 * square)
        pull = half + 0.5 * pre * ((1.0 - bend) * (1.0 + bend)) * inner
        grad_pre = grad_ref[:, start : start + step].astype(F32) * pull
        grad_bias += jnp.sum(grad_pre, axis=1, keepdims=True)
        upper = grad_pre.astype(BF16)
        lower = (grad_pre - upper.astype(F32)).astype(BF16)
        both = lax.dot_general(
            jnp.concatenate([upper, lower], axis=0),
            jnp.concatenate([first, second], axis=0),
            NT,
            preferred_element_type=F32,
        )
        grad_weight += (both[:hidden, depth:] + both[hidden:, :depth]) + both[:hidden, :depth]
    groups = terms_ref.shape[0]
    terms_ref[:, : hidden // groups, :] = grad_weight.reshape(groups, hidden // groups, depth)
    terms_ref[:, hidden // groups :, :] = jnp.broadcast_to(grad_bias, (hidden, depth)).reshape(
        groups, hidden // groups, depth
    )


def layer(aggregated, weight, bias, grad_out, groups):
    depth, nodes = aggregated.shape
    hidden = weight.shape[0]
    vmem = pl.BlockSpec(memory_space=pltpu.VMEM)
    return pl.pallas_call(
        layer_kernel,
        in_specs=[vmem] * 4,
        out_specs=[vmem] * 2,
        out_shape=[
            jax.ShapeDtypeStruct((hidden, nodes), BF16),
            jax.ShapeDtypeStruct((groups, 2 * hidden // groups, depth), F32),
        ],
        compiler_params=pltpu.CompilerParams(vmem_limit_bytes=24 << 20),
        name="layer_and_gradient",
    )(aggregated, weight, bias[:, None], grad_out)


def spread(array, axis):
    size = lax.axis_size(axis)
    return lax.all_to_all(jnp.broadcast_to(array[None], (size,) + array.shape), axis, 0, 0)


def shards(features, keep_cols, send_rows, tile_cols, tile_vals, weight, bias, grad_out):
    feat = lax.axis_size("feat")
    hidden = bias.shape[0]
    kept = keep_cols.shape[0]
    planes = lax.axis_size("z_far")
    near = lax.axis_size(NEAR)
    block = send_rows.shape[2]
    outgoing = keep(keep_cols, features.T, send_rows[0], planes)
    own = outgoing[0, : features.shape[0] // block * kept]
    held = lax.all_to_all(outgoing, "z_far", 0, 0)
    picked = pick(held, near, kept).reshape(near, planes * kept, block)
    incoming = lax.all_to_all(picked, NEAR, 0, 0)
    incoming = incoming.reshape(near, planes, kept, block)
    weight_all = lax.all_gather(weight, "feat", axis=0, tiled=True)
    columns = lax.dynamic_slice_in_dim(weight_all, lax.axis_index("feat") * hidden, hidden, 1).T
    incoming, columns = lax.optimization_barrier((incoming, columns))
    aggregated = aggregate(tile_cols, own, incoming, tile_vals, feat)
    aggregated = lax.all_to_all(aggregated, "feat", 0, 0).reshape(feat * kept, -1)
    groups = lax.axis_size(PLANE)
    out, terms = layer(aggregated, columns, bias, grad_out.T, groups)
    terms = lax.all_to_all(terms, PLANE, 0, 0).sum(axis=0)
    terms = spread(terms, RING).sum(axis=0)
    terms = spread(terms, PLANE)
    rows = hidden // groups
    grad_weight = terms[:, :rows].reshape(hidden, feat * kept)
    grad_bias = terms[:, rows:, 0]
    return out.T, grad_weight.T, grad_bias.reshape(hidden)


def solution(mesh):
    devices = mesh.devices.reshape(4, 4, 4, 2, mesh.shape["feat"])
    fine = Mesh(devices, DOM + ("feat",))
    placed = (
        P(DOM, "feat"),
        P("feat"),
        P(DOM, None, None),
        P(DOM),
        P(DOM, None, None),
        P("feat", None),
        P("feat"),
        P(DOM, "feat"),
    )
    return jax.shard_map(
        shards,
        mesh=fine,
        in_specs=placed,
        out_specs=(P(DOM, "feat"), P(None, "feat"), P("feat")),
        check_vma=False,
    )
```

```python
import functools
import math

import jax
import jax.numpy as jnp
from jax import lax
from jax.experimental import pallas as pl
from jax.experimental.pallas import tpu as pltpu
from jax.sharding import Mesh, PartitionSpec as P

DOM = ("z_far", "z_near", "y", "core")
NEAR = ("z_near", "y", "core")
PLANE = ("y", "core")
RING = ("z_far", "z_near")
NT = (((1,), (1,)), ((), ()))
LOW = 256
CODE = 128
F32 = jnp.float32
BF16 = jnp.bfloat16


def as_column(row):
    size = row.shape[1]
    same = lax.broadcasted_iota(jnp.int32, (size, size), 0) == lax.broadcasted_iota(jnp.int32, (size, size), 1)
    return jnp.sum(jnp.where(same, row, 0.0), axis=1, keepdims=True)


def keep_kernel(keep_ref, features_ref, lists_ref, out_ref):
    planes, rows, block = out_ref.shape
    kept = keep_ref.shape[1]
    nodes = features_ref.shape[1]
    lists = lists_ref.shape[0] // planes
    lane = lax.broadcasted_iota(jnp.int32, (kept, features_ref.shape[0]), 1)
    wanted = as_column(keep_ref[...].astype(F32)).astype(jnp.int32)
    select = jnp.where(lane == wanted, 1.0, 0.0).astype(BF16)
    columns = jnp.dot(select, features_ref[...], preferred_element_type=F32).astype(BF16)
    row = lists_ref[...]
    code = lax.shift_left(CODE + (row & (CODE - 1)), row // CODE)
    code = (code.astype(F32) * (1.0 / CODE)).astype(BF16)
    for plane in range(planes):
        for tile in range(nodes // block):
            out_ref[plane, tile * kept : (tile + 1) * kept, :] = columns[:, tile * block : (tile + 1) * block]
        out_ref[plane, rows - lists :, :] = code[plane * lists : (plane + 1) * lists]


def keep(keep_cols, features, lists, planes):
    peers, block = lists.shape
    nodes = features.shape[1]
    kept = keep_cols.shape[0]
    rows = nodes // block * kept + peers // planes
    vmem = pl.BlockSpec(memory_space=pltpu.VMEM)
    return pl.pallas_call(
        keep_kernel,
        in_specs=[vmem] * 3,
        out_specs=vmem,
        out_shape=jax.ShapeDtypeStruct((planes, rows, block), BF16),
        name="keep_columns",
    )(keep_cols[None, :], features, lists)


def pick_kernel(held_ref, out_ref):
    lists, _, kept, block = out_ref.shape
    tiles = (held_ref.shape[1] - lists) // kept
    span = LOW // block
    highs = tiles // span
    table = jnp.concatenate(
        [
            jnp.concatenate([held_ref[0, t * kept : (t + 1) * kept, :] for t in range(h * span, (h + 1) * span)], axis=1)
            for h in range(highs)
        ],
        axis=0,
    )
    code = (held_ref[0, tiles * kept :, :].astype(F32) * CODE).astype(jnp.int32)
    shift = jnp.zeros((lists, block), jnp.int32)
    for step in range(1, tiles + 1):
        shift += jnp.where(code >= CODE << step, 1, 0)
    row = shift * CODE + (lax.shift_right_logical(code, shift) - CODE)
    sub = lax.broadcasted_iota(jnp.int32, (LOW, 2 * block), 0)
    for pair in range(lists // 2):
        rows = jnp.concatenate([row[2 * pair : 2 * pair + 1, :], row[2 * pair + 1 : 2 * pair + 2, :]], axis=1)
        low = rows & (LOW - 1)
        high = rows // LOW
        onehot = jnp.where(sub == low, 1.0, 0.0).astype(BF16)
        found = jnp.dot(table, onehot, preferred_element_type=F32)
        total = jnp.zeros((kept, 2 * block), F32)
        for step in range(highs):
            total = jnp.where(high == step, found[step * kept : (step + 1) * kept], total)
        total = total.astype(BF16)
        out_ref[2 * pair, 0] = total[:, :block]
        out_ref[2 * pair + 1, 0] = total[:, block:]


def pick(held, lists, kept):
    planes, rows, block = held.shape
    return pl.pallas_call(
        pick_kernel,
        grid=(planes,),
        in_specs=[pl.BlockSpec((1, rows, block), lambda i: (i, 0, 0))],
        out_specs=pl.BlockSpec((lists, 1, kept, block), lambda i: (0, i, 0, 0)),
        out_shape=jax.ShapeDtypeStruct((lists, planes, kept, block), BF16),
        compiler_params=pltpu.CompilerParams(vmem_limit_bytes=24 << 20),
        name="pick_rows",
    )(held)


def aggregate_kernel(tiles_row, cols_ref, own_ref, incoming_ref, vals_ref, out_ref):
    kept, block = incoming_ref.shape[1:]
    own = vals_ref.shape[0] // tiles_row
    for tile in range(vals_ref.shape[0] // tiles_row):
        values, picked = [], []
        for term in range(tiles_row):
            at = tile * tiles_row + term
            column = cols_ref[at]
            mine = own_ref[pl.ds(pl.multiple_of(jnp.minimum(column, own - 1) * kept, kept), kept), :]
            theirs = incoming_ref[jnp.maximum(column - own, 0)]
            picked.append(jnp.where(column < own, mine, theirs))
            values.append(vals_ref[at])
        total = lax.dot_general(
            jnp.concatenate(picked, axis=1), jnp.concatenate(values, axis=1), NT, preferred_element_type=F32
        )
        for copy in range(out_ref.shape[0]):
            out_ref[copy, :, tile * block : (tile + 1) * block] = total


def aggregate(tile_cols, own, incoming, tile_vals, copies):
    kept, block = incoming.shape[1:]
    tiles = own.shape[0] // kept
    vmem = pl.BlockSpec(memory_space=pltpu.VMEM)
    return pl.pallas_call(
        functools.partial(aggregate_kernel, tile_cols.shape[0] // tiles),
        in_specs=[pl.BlockSpec(memory_space=pltpu.SMEM), vmem, vmem, vmem],
        out_specs=vmem,
        out_shape=jax.ShapeDtypeStruct((copies, kept, tiles * block), F32),
        compiler_params=pltpu.CompilerParams(vmem_limit_bytes=24 << 20),
        name="aggregate_tiles",
    )(tile_cols, own, incoming, tile_vals)


def layer_kernel(agg_ref, weight_ref, bias_ref, grad_ref, out_ref, terms_ref):
    hidden, nodes = grad_ref.shape
    step = 256
    depth = agg_ref.shape[0]
    slope = math.sqrt(2.0 / math.pi)
    weight = jnp.concatenate([weight_ref[...]] * 3, axis=1)
    bias = jnp.concatenate([bias_ref[...]] * (step // bias_ref.shape[1]), axis=1)
    grad_weight = jnp.zeros((hidden, depth), F32)
    grad_bias = jnp.zeros((hidden, 1), F32)
    for start in range(0, nodes, step):
        exact = agg_ref[:, start : start + step]
        first = exact.astype(BF16)
        rest = exact - first.astype(F32)
        second = rest.astype(BF16)
        third = (rest - second.astype(F32)).astype(BF16)
        pre = jnp.dot(weight, jnp.concatenate([first, second, third], axis=0), preferred_element_type=F32)
        pre = pre + bias
        square = pre * pre
        bend = jnp.tanh(slope * (pre + 0.044715 * (pre * square)))
        half = 0.5 * (1.0 + bend)
        out_ref[:, start : start + step] = (pre * half).astype(BF16)
        inner = slope * (1.0 + 3 * 0.044715 * square)
        pull = half + 0.5 * pre * ((1.0 - bend) * (1.0 + bend)) * inner
        grad_pre = grad_ref[:, start : start + step].astype(F32) * pull
        grad_bias += jnp.sum(grad_pre, axis=1, keepdims=True)
        upper = grad_pre.astype(BF16)
        lower = (grad_pre - upper.astype(F32)).astype(BF16)
        both = lax.dot_general(
            jnp.concatenate([upper, lower], axis=0),
            jnp.concatenate([first, second], axis=0),
            NT,
            preferred_element_type=F32,
        )
        grad_weight += (both[:hidden, depth:] + both[hidden:, :depth]) + both[:hidden, :depth]
    groups = terms_ref.shape[0]
    rows = hidden // groups
    lane = lax.broadcasted_iota(jnp.int32, (hidden, depth), 1)
    spot = lax.broadcasted_iota(jnp.int32, (hidden, depth), 0)
    diagonal = jnp.where(lane == spot, grad_bias, 0.0).reshape(groups, rows, depth)
    terms_ref[:, :rows, :] = grad_weight.reshape(groups, rows, depth)
    terms_ref[:, rows:, :] = jnp.broadcast_to(jnp.sum(diagonal, axis=1, keepdims=True), (groups, rows, depth))


def layer(aggregated, weight, bias, grad_out, groups):
    depth, nodes = aggregated.shape
    hidden = weight.shape[0]
    vmem = pl.BlockSpec(memory_space=pltpu.VMEM)
    return pl.pallas_call(
        layer_kernel,
        in_specs=[vmem] * 4,
        out_specs=[vmem] * 2,
        out_shape=[
            jax.ShapeDtypeStruct((hidden, nodes), BF16),
            jax.ShapeDtypeStruct((groups, 2 * hidden // groups, depth), F32),
        ],
        compiler_params=pltpu.CompilerParams(vmem_limit_bytes=24 << 20),
        name="layer_and_gradient",
    )(aggregated, weight, bias, grad_out)


def unpack_kernel(terms_ref, weight_ref, bias_ref):
    groups = terms_ref.shape[0]
    hidden, depth = weight_ref.shape
    rows = hidden // groups
    weight_ref[...] = terms_ref[:, :rows, :].reshape(hidden, depth)
    bias_ref[...] = jnp.sum(terms_ref[:, rows : rows + 1, :], axis=0)[:, :hidden]


def unpack(terms, hidden):
    depth = terms.shape[2]
    vmem = pl.BlockSpec(memory_space=pltpu.VMEM)
    return pl.pallas_call(
        unpack_kernel,
        in_specs=[vmem],
        out_specs=[vmem] * 2,
        out_shape=[jax.ShapeDtypeStruct((hidden, depth), F32), jax.ShapeDtypeStruct((1, hidden), F32)],
        compiler_params=pltpu.CompilerParams(vmem_limit_bytes=24 << 20),
        name="unpack_gradients",
    )(terms)


def spread(array, axis):
    size = lax.axis_size(axis)
    return lax.all_to_all(jnp.broadcast_to(array[None], (size,) + array.shape), axis, 0, 0)


def shards(features, keep_cols, send_rows, tile_cols, tile_vals, weight, bias, grad_out):
    feat = lax.axis_size("feat")
    hidden = bias.shape[0]
    kept = keep_cols.shape[0]
    planes = lax.axis_size("z_far")
    near = lax.axis_size(NEAR)
    block = send_rows.shape[2]
    outgoing = keep(keep_cols, features.T, send_rows[0], planes)
    own = outgoing[0, : features.shape[0] // block * kept]
    held = lax.all_to_all(outgoing, "z_far", 0, 0)
    picked = pick(held, near, kept).reshape(near, planes * kept, block)
    incoming = lax.all_to_all(picked, NEAR, 0, 0)
    incoming = incoming.reshape(near * planes, kept, block)
    tiles = features.shape[0] // block
    sender = tile_cols - tiles
    place = tiles + lax.rem(sender, near) * planes + lax.div(sender, near)
    tile_cols = jnp.where(sender < 0, tile_cols, place)
    bias = jnp.broadcast_to(bias[:, None], (hidden, block))
    weight_all = lax.all_gather(weight, "feat", axis=0, tiled=True)
    columns = lax.dynamic_slice_in_dim(weight_all, lax.axis_index("feat") * hidden, hidden, 1).T
    incoming, columns, tile_cols, bias = lax.optimization_barrier((incoming, columns, tile_cols, bias))
    aggregated = aggregate(tile_cols, own, incoming, tile_vals, feat)
    aggregated = lax.all_to_all(aggregated, "feat", 0, 0).reshape(feat * kept, -1)
    groups = lax.axis_size(PLANE)
    out, terms = layer(aggregated, columns, bias, grad_out.T, groups)
    terms = lax.all_to_all(terms, PLANE, 0, 0).sum(axis=0)
    rows = hidden // groups + 1
    packed = spread(terms[:rows].reshape(1, -1), RING).sum(axis=0).reshape(rows, -1)
    terms = spread(jnp.pad(packed, ((0, terms.shape[0] - rows), (0, 0))), PLANE)
    grad_weight, grad_bias = unpack(terms, hidden)
    return out.T, grad_weight.T, grad_bias.reshape(hidden)


def solution(mesh):
    devices = mesh.devices.reshape(4, 4, 4, 2, mesh.shape["feat"])
    fine = Mesh(devices, DOM + ("feat",))
    placed = (
        P(DOM, "feat"),
        P("feat"),
        P(DOM, None, None),
        P(DOM),
        P(DOM, None, None),
        P("feat", None),
        P("feat"),
        P(DOM, "feat"),
    )
    return jax.shard_map(
        shards,
        mesh=fine,
        in_specs=placed,
        out_specs=(P(DOM, "feat"), P(None, "feat"), P("feat")),
        check_vma=False,
    )
```

```python
import functools
import math

import jax
import jax.numpy as jnp
from jax import lax
from jax.experimental import pallas as pl
from jax.experimental.pallas import tpu as pltpu
from jax.sharding import Mesh, PartitionSpec as P

DOM = ("z_far", "z_near", "y", "core")
NEAR = ("z_near", "y", "core")
PLANE = ("y", "core")
RING = ("z_far", "z_near")
NT = (((1,), (1,)), ((), ()))
LOW = 256
CODE = 128
ORDER = (2, 1, 3)
F32 = jnp.float32
BF16 = jnp.bfloat16


def as_column(row):
    size = row.shape[1]
    same = lax.broadcasted_iota(jnp.int32, (size, size), 0) == lax.broadcasted_iota(jnp.int32, (size, size), 1)
    return jnp.sum(jnp.where(same, row, 0.0), axis=1, keepdims=True)


def keep_kernel(keep_ref, features_ref, lists_ref, *refs):
    out_refs, code_ref = refs[:-1], refs[-1]
    planes = len(out_refs)
    rows, block = out_refs[0].shape
    kept = keep_ref.shape[1]
    nodes = features_ref.shape[1]
    lists = lists_ref.shape[0] // planes
    lane = lax.broadcasted_iota(jnp.int32, (kept, features_ref.shape[0]), 1)
    wanted = as_column(keep_ref[...].astype(F32)).astype(jnp.int32)
    select = jnp.where(lane == wanted, 1.0, 0.0).astype(BF16)
    columns = jnp.dot(select, features_ref[...], preferred_element_type=F32).astype(BF16)
    row = lists_ref[...]
    code = lax.shift_left(CODE + (row & (CODE - 1)), row // CODE)
    code_ref[...] = (code.astype(F32) * (1.0 / CODE)).astype(BF16)
    me = lax.axis_index("z_far")
    for ahead, out_ref in enumerate(out_refs):
        for tile in range(nodes // block):
            out_ref[tile * kept : (tile + 1) * kept, :] = columns[:, tile * block : (tile + 1) * block]
        first = pl.multiple_of(lax.rem(me + ahead, planes) * lists, lists)
        out_ref[rows - lists :, :] = code_ref[pl.ds(first, lists), :]


def keep(keep_cols, features, lists, planes):
    peers, block = lists.shape
    nodes = features.shape[1]
    kept = keep_cols.shape[0]
    rows = nodes // block * kept + peers // planes
    vmem = pl.BlockSpec(memory_space=pltpu.VMEM)
    return pl.pallas_call(
        keep_kernel,
        in_specs=[vmem] * 3,
        out_specs=[vmem] * planes,
        out_shape=[jax.ShapeDtypeStruct((rows, block), BF16)] * planes,
        scratch_shapes=[pltpu.VMEM(lists.shape, BF16)],
        name="keep_columns",
    )(keep_cols[None, :], features, lists)


def pick_kernel(held_ref, *rest):
    out_ref = rest[-1]
    lists, _, kept, block = out_ref.shape
    tiles = (held_ref.shape[0] - lists) // kept
    span = LOW // block
    highs = tiles // span
    table = jnp.concatenate(
        [
            jnp.concatenate([held_ref[t * kept : (t + 1) * kept, :] for t in range(h * span, (h + 1) * span)], axis=1)
            for h in range(highs)
        ],
        axis=0,
    )
    code = (held_ref[tiles * kept :, :].astype(F32) * CODE).astype(jnp.int32)
    shift = jnp.zeros((lists, block), jnp.int32)
    for step in range(1, tiles + 1):
        shift += jnp.where(code >= CODE << step, 1, 0)
    row = shift * CODE + (lax.shift_right_logical(code, shift) - CODE)
    sub = lax.broadcasted_iota(jnp.int32, (LOW, 2 * block), 0).astype(F32).astype(BF16)
    for pair in range(lists // 2):
        rows = jnp.concatenate([row[2 * pair : 2 * pair + 1, :], row[2 * pair + 1 : 2 * pair + 2, :]], axis=1)
        low = (rows & (LOW - 1)).astype(F32).astype(BF16)
        high = rows // LOW
        onehot = jnp.where(sub == low, jnp.ones((), BF16), jnp.zeros((), BF16))
        found = jnp.dot(table, onehot, preferred_element_type=F32)
        total = jnp.zeros((kept, 2 * block), F32)
        for step in range(highs):
            total = jnp.where(high == step, found[step * kept : (step + 1) * kept], total)
        total = total.astype(BF16)
        out_ref[2 * pair, 0] = total[:, :block]
        out_ref[2 * pair + 1, 0] = total[:, block:]


def pick(held, part, parts, lists, kept, before):
    rows, block = held.shape
    earlier = [] if before is None else [before]
    return pl.pallas_call(
        pick_kernel,
        grid=(1,),
        in_specs=[pl.BlockSpec((rows, block), lambda i: (0, 0))]
        + [pl.BlockSpec(memory_space=pl.ANY)] * len(earlier),
        out_specs=pl.BlockSpec((lists, 1, kept, block), lambda i: (0, part, 0, 0)),
        out_shape=jax.ShapeDtypeStruct((lists, parts, kept, block), BF16),
        input_output_aliases={1: 0} if earlier else {},
        compiler_params=pltpu.CompilerParams(vmem_limit_bytes=24 << 20),
        cost_estimate=pl.CostEstimate(
            flops=2 * lists * block * LOW * block, bytes_accessed=2 * block * (lists * kept + rows), transcendentals=0
        ),
        name="pick_rows",
    )(held, *earlier)


def aggregate_kernel(tiles_row, cols_ref, own_ref, incoming_ref, vals_ref, out_ref):
    kept, block = incoming_ref.shape[1:]
    own = vals_ref.shape[0] // tiles_row
    for tile in range(vals_ref.shape[0] // tiles_row):
        values, picked = [], []
        for term in range(tiles_row):
            at = tile * tiles_row + term
            column = cols_ref[at]
            mine = own_ref[pl.ds(pl.multiple_of(jnp.minimum(column, own - 1) * kept, kept), kept), :]
            theirs = incoming_ref[jnp.maximum(column - own, 0)]
            picked.append(jnp.where(column < own, mine, theirs))
            values.append(vals_ref[at])
        total = lax.dot_general(
            jnp.concatenate(picked, axis=1), jnp.concatenate(values, axis=1), NT, preferred_element_type=F32
        )
        for copy in range(out_ref.shape[0]):
            out_ref[copy, :, tile * block : (tile + 1) * block] = total


def aggregate(tile_cols, own, incoming, tile_vals, copies):
    kept, block = incoming.shape[1:]
    tiles = own.shape[0] // kept
    vmem = pl.BlockSpec(memory_space=pltpu.VMEM)
    return pl.pallas_call(
        functools.partial(aggregate_kernel, tile_cols.shape[0] // tiles),
        in_specs=[pl.BlockSpec(memory_space=pltpu.SMEM), vmem, vmem, vmem],
        out_specs=vmem,
        out_shape=jax.ShapeDtypeStruct((copies, kept, tiles * block), F32),
        compiler_params=pltpu.CompilerParams(vmem_limit_bytes=24 << 20),
        name="aggregate_tiles",
    )(tile_cols, own, incoming, tile_vals)


def layer_kernel(agg_ref, weight_ref, bias_ref, grad_ref, out_ref, terms_ref):
    hidden, nodes = grad_ref.shape
    step = 256
    depth = agg_ref.shape[0]
    slope = math.sqrt(2.0 / math.pi)
    weight = jnp.concatenate([weight_ref[...]] * 3, axis=1)
    bias = jnp.concatenate([bias_ref[...]] * (step // bias_ref.shape[1]), axis=1)
    grad_weight = jnp.zeros((hidden, depth), F32)
    grad_bias = jnp.zeros((hidden, 1), F32)
    for start in range(0, nodes, step):
        exact = agg_ref[:, start : start + step]
        first = exact.astype(BF16)
        rest = exact - first.astype(F32)
        second = rest.astype(BF16)
        third = (rest - second.astype(F32)).astype(BF16)
        pre = jnp.dot(weight, jnp.concatenate([first, second, third], axis=0), preferred_element_type=F32)
        pre = pre + bias
        square = pre * pre
        bend = jnp.tanh(slope * (pre + 0.044715 * (pre * square)))
        half = 0.5 * (1.0 + bend)
        out_ref[:, start : start + step] = (pre * half).astype(BF16)
        inner = slope * (1.0 + 3 * 0.044715 * square)
        pull = half + 0.5 * pre * ((1.0 - bend) * (1.0 + bend)) * inner
        grad_pre = grad_ref[:, start : start + step].astype(F32) * pull
        grad_bias += jnp.sum(grad_pre, axis=1, keepdims=True)
        upper = grad_pre.astype(BF16)
        lower = (grad_pre - upper.astype(F32)).astype(BF16)
        both = lax.dot_general(
            jnp.concatenate([upper, lower], axis=0),
            jnp.concatenate([first, second], axis=0),
            NT,
            preferred_element_type=F32,
        )
        grad_weight += (both[:hidden, depth:] + both[hidden:, :depth]) + both[:hidden, :depth]
    groups = terms_ref.shape[0]
    rows = hidden // groups
    lane = lax.broadcasted_iota(jnp.int32, (hidden, depth), 1)
    spot = lax.broadcasted_iota(jnp.int32, (hidden, depth), 0)
    diagonal = jnp.where(lane == spot, grad_bias, 0.0).reshape(groups, rows, depth)
    terms_ref[:, :rows, :] = grad_weight.reshape(groups, rows, depth)
    terms_ref[:, rows:, :] = jnp.broadcast_to(jnp.sum(diagonal, axis=1, keepdims=True), (groups, rows, depth))


def layer(aggregated, weight, bias, grad_out, groups):
    depth, nodes = aggregated.shape
    hidden = weight.shape[0]
    vmem = pl.BlockSpec(memory_space=pltpu.VMEM)
    return pl.pallas_call(
        layer_kernel,
        in_specs=[vmem] * 4,
        out_specs=[vmem] * 2,
        out_shape=[
            jax.ShapeDtypeStruct((hidden, nodes), BF16),
            jax.ShapeDtypeStruct((groups, 2 * hidden // groups, depth), F32),
        ],
        compiler_params=pltpu.CompilerParams(vmem_limit_bytes=24 << 20),
        name="layer_and_gradient",
    )(aggregated, weight, bias, grad_out)


def unpack_kernel(terms_ref, weight_ref, bias_ref):
    groups = terms_ref.shape[0]
    hidden, depth = weight_ref.shape
    rows = hidden // groups
    weight_ref[...] = terms_ref[:, :rows, :].reshape(hidden, depth)
    bias_ref[...] = jnp.sum(terms_ref[:, rows : rows + 1, :], axis=0)[:, :hidden]


def unpack(terms, hidden):
    depth = terms.shape[2]
    vmem = pl.BlockSpec(memory_space=pltpu.VMEM)
    return pl.pallas_call(
        unpack_kernel,
        in_specs=[vmem],
        out_specs=[vmem] * 2,
        out_shape=[jax.ShapeDtypeStruct((hidden, depth), F32), jax.ShapeDtypeStruct((1, hidden), F32)],
        compiler_params=pltpu.CompilerParams(vmem_limit_bytes=24 << 20),
        name="unpack_gradients",
    )(terms)


def spread(array, axis):
    size = lax.axis_size(axis)
    return lax.all_to_all(jnp.broadcast_to(array[None], (size,) + array.shape), axis, 0, 0)


def shards(features, keep_cols, send_rows, tile_cols, tile_vals, weight, bias, grad_out):
    feat = lax.axis_size("feat")
    hidden = bias.shape[0]
    kept = keep_cols.shape[0]
    planes = lax.axis_size("z_far")
    near = lax.axis_size(NEAR)
    block = send_rows.shape[2]
    outgoing = keep(keep_cols, features.T, send_rows[0], planes)
    own = outgoing[0][: features.shape[0] // block * kept]
    held = [outgoing[0]] + [None] * (planes - 1)
    for ahead in ORDER:
        held[ahead] = lax.ppermute(outgoing[ahead], "z_far", [(i, (i + ahead) % planes) for i in range(planes)])
    picked = None
    for ahead in (0,) + ORDER:
        picked = pick(held[ahead], ahead, planes, near, kept, picked)
    picked = picked.reshape(near, planes * kept, block)
    incoming = lax.all_to_all(picked, NEAR, 0, 0)
    incoming = incoming.reshape(near * planes, kept, block)
    tiles = features.shape[0] // block
    sender = tile_cols - tiles
    behind = lax.rem(lax.axis_index("z_far") + planes - lax.div(sender, near), planes)
    place = tiles + lax.rem(sender, near) * planes + behind
    tile_cols = jnp.where(sender < 0, tile_cols, place)
    bias = jnp.broadcast_to(bias[:, None], (hidden, block))
    weight_all = lax.all_gather(weight, "feat", axis=0, tiled=True)
    columns = lax.dynamic_slice_in_dim(weight_all, lax.axis_index("feat") * hidden, hidden, 1).T
    incoming, columns, tile_cols, bias = lax.optimization_barrier((incoming, columns, tile_cols, bias))
    aggregated = aggregate(tile_cols, own, incoming, tile_vals, feat)
    aggregated = lax.all_to_all(aggregated, "feat", 0, 0).reshape(feat * kept, -1)
    groups = lax.axis_size(PLANE)
    out, terms = layer(aggregated, columns, bias, grad_out.T, groups)
    terms = lax.all_to_all(terms, PLANE, 0, 0).sum(axis=0)
    rows = hidden // groups + 1
    packed = spread(terms[:rows].reshape(1, -1), RING).sum(axis=0).reshape(rows, -1)
    terms = spread(jnp.pad(packed, ((0, terms.shape[0] - rows), (0, 0))), PLANE)
    grad_weight, grad_bias = unpack(terms, hidden)
    return out.T, grad_weight.T, grad_bias.reshape(hidden)


def solution(mesh):
    devices = mesh.devices.reshape(4, 4, 4, 2, mesh.shape["feat"])
    fine = Mesh(devices, DOM + ("feat",))
    placed = (
        P(DOM, "feat"),
        P("feat"),
        P(DOM, None, None),
        P(DOM),
        P(DOM, None, None),
        P("feat", None),
        P("feat"),
        P(DOM, "feat"),
    )
    return jax.shard_map(
        shards,
        mesh=fine,
        in_specs=placed,
        out_specs=(P(DOM, "feat"), P(None, "feat"), P("feat")),
        check_vma=False,
    )
```

```python
import functools
import math

import jax
import jax.numpy as jnp
from jax import lax
from jax.experimental import pallas as pl
from jax.experimental.pallas import tpu as pltpu
from jax.sharding import Mesh, PartitionSpec as P

DOM = ("z_far", "z_near", "y", "core")
NEAR = ("z_near", "y", "core")
PLANE = ("y", "core")
RING = ("z_far", "z_near")
NT = (((1,), (1,)), ((), ()))
LOW = 256
CODE = 128
ORDER = (2, 1, 3)
F32 = jnp.float32
BF16 = jnp.bfloat16


def as_column(row):
    size = row.shape[1]
    same = lax.broadcasted_iota(jnp.int32, (size, size), 0) == lax.broadcasted_iota(jnp.int32, (size, size), 1)
    return jnp.sum(jnp.where(same, row, 0.0), axis=1, keepdims=True)


def keep_kernel(keep_ref, features_ref, lists_ref, *refs):
    out_refs, code_ref = refs[:-1], refs[-1]
    planes = len(out_refs)
    rows, block = out_refs[0].shape
    kept = keep_ref.shape[1]
    nodes = features_ref.shape[1]
    lists = lists_ref.shape[0] // planes
    lane = lax.broadcasted_iota(jnp.int32, (kept, features_ref.shape[0]), 1)
    wanted = as_column(keep_ref[...].astype(F32)).astype(jnp.int32)
    select = jnp.where(lane == wanted, 1.0, 0.0).astype(BF16)
    columns = jnp.dot(select, features_ref[...], preferred_element_type=F32).astype(BF16)
    row = lists_ref[...]
    code = lax.shift_left(CODE + (row & (CODE - 1)), row // CODE)
    code_ref[...] = (code.astype(F32) * (1.0 / CODE)).astype(BF16)
    me = lax.axis_index("z_far")
    for ahead, out_ref in enumerate(out_refs):
        for tile in range(nodes // block):
            out_ref[tile * kept : (tile + 1) * kept, :] = columns[:, tile * block : (tile + 1) * block]
        first = pl.multiple_of(lax.rem(me + ahead, planes) * lists, lists)
        out_ref[rows - lists :, :] = code_ref[pl.ds(first, lists), :]


def keep(keep_cols, features, lists, planes):
    peers, block = lists.shape
    nodes = features.shape[1]
    kept = keep_cols.shape[0]
    rows = nodes // block * kept + peers // planes
    vmem = pl.BlockSpec(memory_space=pltpu.VMEM)
    return pl.pallas_call(
        keep_kernel,
        in_specs=[vmem] * 3,
        out_specs=[vmem] * planes,
        out_shape=[jax.ShapeDtypeStruct((rows, block), BF16)] * planes,
        scratch_shapes=[pltpu.VMEM(lists.shape, BF16)],
        name="keep_columns",
    )(keep_cols[None, :], features, lists)


def pick_kernel(held_ref, *rest):
    out_ref = rest[-1]
    lists, _, kept, block = out_ref.shape
    tiles = (held_ref.shape[0] - lists) // kept
    span = LOW // block
    highs = tiles // span
    table = jnp.concatenate(
        [
            jnp.concatenate([held_ref[t * kept : (t + 1) * kept, :] for t in range(h * span, (h + 1) * span)], axis=1)
            for h in range(highs)
        ],
        axis=0,
    )
    code = (held_ref[tiles * kept :, :].astype(F32) * CODE).astype(jnp.int32)
    shift = jnp.zeros((lists, block), jnp.int32)
    for step in range(1, tiles + 1):
        shift += jnp.where(code >= CODE << step, 1, 0)
    row = shift * CODE + (lax.shift_right_logical(code, shift) - CODE)
    sub = lax.broadcasted_iota(jnp.int32, (LOW, 2 * block), 0).astype(F32).astype(BF16)
    for pair in range(lists // 2):
        rows = jnp.concatenate([row[2 * pair : 2 * pair + 1, :], row[2 * pair + 1 : 2 * pair + 2, :]], axis=1)
        low = (rows & (LOW - 1)).astype(F32).astype(BF16)
        high = rows // LOW
        onehot = jnp.where(sub == low, jnp.ones((), BF16), jnp.zeros((), BF16))
        found = jnp.dot(table, onehot, preferred_element_type=F32)
        total = jnp.zeros((kept, 2 * block), F32)
        for step in range(highs):
            total = jnp.where(high == step, found[step * kept : (step + 1) * kept], total)
        total = total.astype(BF16)
        out_ref[2 * pair, 0] = total[:, :block]
        out_ref[2 * pair + 1, 0] = total[:, block:]


def pick(held, part, parts, lists, kept, before):
    rows, block = held.shape
    earlier = [] if before is None else [before]
    return pl.pallas_call(
        pick_kernel,
        grid=(1,),
        in_specs=[pl.BlockSpec((rows, block), lambda i: (0, 0))]
        + [pl.BlockSpec(memory_space=pl.ANY)] * len(earlier),
        out_specs=pl.BlockSpec((lists, 1, kept, block), lambda i: (0, part, 0, 0)),
        out_shape=jax.ShapeDtypeStruct((lists, parts, kept, block), BF16),
        input_output_aliases={1: 0} if earlier else {},
        compiler_params=pltpu.CompilerParams(vmem_limit_bytes=24 << 20),
        cost_estimate=pl.CostEstimate(
            flops=2 * lists * block * LOW * block, bytes_accessed=2 * block * (lists * kept + rows), transcendentals=0
        ),
        name="pick_rows",
    )(held, *earlier)


def aggregate_kernel(tiles_row, cols_ref, own_ref, incoming_ref, vals_ref, out_ref):
    kept, block = incoming_ref.shape[1:]
    own = vals_ref.shape[0] // tiles_row
    for tile in range(vals_ref.shape[0] // tiles_row):
        values, picked = [], []
        for term in range(tiles_row):
            at = tile * tiles_row + term
            column = cols_ref[at]
            mine = own_ref[pl.ds(pl.multiple_of(jnp.minimum(column, own - 1) * kept, kept), kept), :]
            theirs = incoming_ref[jnp.maximum(column - own, 0)]
            picked.append(jnp.where(column < own, mine, theirs))
            values.append(vals_ref[at])
        total = lax.dot_general(
            jnp.concatenate(picked, axis=1), jnp.concatenate(values, axis=1), NT, preferred_element_type=F32
        )
        for copy in range(out_ref.shape[0]):
            out_ref[copy, :, tile * block : (tile + 1) * block] = total


def aggregate(tile_cols, own, incoming, tile_vals, copies):
    kept, block = incoming.shape[1:]
    tiles = own.shape[0] // kept
    vmem = pl.BlockSpec(memory_space=pltpu.VMEM)
    return pl.pallas_call(
        functools.partial(aggregate_kernel, tile_cols.shape[0] // tiles),
        in_specs=[pl.BlockSpec(memory_space=pltpu.SMEM), vmem, vmem, vmem],
        out_specs=vmem,
        out_shape=jax.ShapeDtypeStruct((copies, kept, tiles * block), F32),
        compiler_params=pltpu.CompilerParams(vmem_limit_bytes=24 << 20),
        name="aggregate_tiles",
    )(tile_cols, own, incoming, tile_vals)


def layer_kernel(agg_ref, weight_ref, grad_ref, out_ref, terms_ref):
    hidden, nodes = grad_ref.shape
    step = 256
    depth = agg_ref.shape[0]
    slope = math.sqrt(2.0 / math.pi)
    weight = jnp.concatenate([weight_ref[:, :depth].astype(BF16)] * 3, axis=1)
    bias = jnp.concatenate([weight_ref[:, depth:]] * (step // depth), axis=1)
    grad_weight = jnp.zeros((hidden, depth), F32)
    grad_bias = jnp.zeros((hidden, 1), F32)
    for start in range(0, nodes, step):
        exact = agg_ref[:, start : start + step]
        first = exact.astype(BF16)
        rest = exact - first.astype(F32)
        second = rest.astype(BF16)
        third = (rest - second.astype(F32)).astype(BF16)
        pre = jnp.dot(weight, jnp.concatenate([first, second, third], axis=0), preferred_element_type=F32)
        pre = pre + bias
        square = pre * pre
        bend = jnp.tanh(slope * (pre + 0.044715 * (pre * square)))
        half = 0.5 * (1.0 + bend)
        out_ref[:, start : start + step] = (pre * half).astype(BF16)
        inner = slope * (1.0 + 3 * 0.044715 * square)
        pull = half + 0.5 * pre * ((1.0 - bend) * (1.0 + bend)) * inner
        grad_pre = grad_ref[:, start : start + step].astype(F32) * pull
        grad_bias += jnp.sum(grad_pre, axis=1, keepdims=True)
        upper = grad_pre.astype(BF16)
        lower = (grad_pre - upper.astype(F32)).astype(BF16)
        both = lax.dot_general(
            jnp.concatenate([upper, lower], axis=0),
            jnp.concatenate([first, second], axis=0),
            NT,
            preferred_element_type=F32,
        )
        grad_weight += (both[:hidden, depth:] + both[hidden:, :depth]) + both[:hidden, :depth]
    groups = terms_ref.shape[0]
    rows = hidden // groups
    lane = lax.broadcasted_iota(jnp.int32, (hidden, depth), 1)
    spot = lax.broadcasted_iota(jnp.int32, (hidden, depth), 0)
    diagonal = jnp.where(lane == spot, grad_bias, 0.0).reshape(groups, rows, depth)
    terms_ref[:, :rows, :] = grad_weight.reshape(groups, rows, depth)
    terms_ref[:, rows:, :] = jnp.broadcast_to(jnp.sum(diagonal, axis=1, keepdims=True), (groups, rows, depth))


def layer(aggregated, weight, grad_out, groups):
    depth, nodes = aggregated.shape
    hidden = weight.shape[0]
    vmem = pl.BlockSpec(memory_space=pltpu.VMEM)
    return pl.pallas_call(
        layer_kernel,
        in_specs=[vmem] * 3,
        out_specs=[vmem] * 2,
        out_shape=[
            jax.ShapeDtypeStruct((hidden, nodes), BF16),
            jax.ShapeDtypeStruct((groups, 2 * hidden // groups, depth), F32),
        ],
        compiler_params=pltpu.CompilerParams(vmem_limit_bytes=24 << 20),
        name="layer_and_gradient",
    )(aggregated, weight, grad_out)


def unpack_kernel(terms_ref, weight_ref, bias_ref):
    groups = terms_ref.shape[0]
    hidden, depth = weight_ref.shape
    rows = hidden // groups
    weight_ref[...] = terms_ref[:, :rows, :].reshape(hidden, depth)
    bias_ref[...] = jnp.sum(terms_ref[:, rows : rows + 1, :], axis=0)[:, :hidden]


def unpack(terms, hidden):
    depth = terms.shape[2]
    vmem = pl.BlockSpec(memory_space=pltpu.VMEM)
    return pl.pallas_call(
        unpack_kernel,
        in_specs=[vmem],
        out_specs=[vmem] * 2,
        out_shape=[jax.ShapeDtypeStruct((hidden, depth), F32), jax.ShapeDtypeStruct((1, hidden), F32)],
        compiler_params=pltpu.CompilerParams(vmem_limit_bytes=24 << 20),
        name="unpack_gradients",
    )(terms)


def spread(array, axis):
    size = lax.axis_size(axis)
    return lax.all_to_all(jnp.broadcast_to(array[None], (size,) + array.shape), axis, 0, 0)


def shards(features, keep_cols, send_rows, tile_cols, tile_vals, weight, bias, grad_out):
    feat = lax.axis_size("feat")
    hidden = bias.shape[0]
    kept = keep_cols.shape[0]
    planes = lax.axis_size("z_far")
    near = lax.axis_size(NEAR)
    block = send_rows.shape[2]
    outgoing = keep(keep_cols, features.T, send_rows[0], planes)
    own = outgoing[0][: features.shape[0] // block * kept]
    held = [outgoing[0]] + [None] * (planes - 1)
    for ahead in ORDER:
        held[ahead] = lax.ppermute(outgoing[ahead], "z_far", [(i, (i + ahead) % planes) for i in range(planes)])
    picked = None
    for ahead in (0,) + ORDER:
        picked = pick(held[ahead], ahead, planes, near, kept, picked)
    picked = picked.reshape(near, planes * kept, block)
    incoming = lax.all_to_all(picked, NEAR, 0, 0)
    incoming = incoming.reshape(near * planes, kept, block)
    tiles = features.shape[0] // block
    sender = tile_cols - tiles
    behind = lax.rem(lax.axis_index("z_far") + planes - lax.div(sender, near), planes)
    place = tiles + lax.rem(sender, near) * planes + behind
    tile_cols = jnp.where(sender < 0, tile_cols, place)
    weight_all = lax.all_gather(weight, "feat", axis=0, tiled=True)
    columns = lax.dynamic_slice_in_dim(weight_all, lax.axis_index("feat") * hidden, hidden, 1).T
    bias = jnp.broadcast_to(bias[:, None], columns.shape)
    columns = jnp.concatenate([columns.astype(F32), bias], axis=1)
    incoming, columns, tile_cols = lax.optimization_barrier((incoming, columns, tile_cols))
    aggregated = aggregate(tile_cols, own, incoming, tile_vals, feat)
    aggregated = lax.all_to_all(aggregated, "feat", 0, 0).reshape(feat * kept, -1)
    groups = lax.axis_size(PLANE)
    out, terms = layer(aggregated, columns, grad_out.T, groups)
    terms = lax.all_to_all(terms, PLANE, 0, 0).sum(axis=0)
    rows = hidden // groups + 1
    packed = spread(terms[:rows].reshape(1, -1), RING).sum(axis=0).reshape(rows, -1)
    terms = spread(jnp.pad(packed, ((0, terms.shape[0] - rows), (0, 0))), PLANE)
    grad_weight, grad_bias = unpack(terms, hidden)
    return out.T, grad_weight.T, grad_bias.reshape(hidden)


def solution(mesh):
    devices = mesh.devices.reshape(4, 4, 4, 2, mesh.shape["feat"])
    fine = Mesh(devices, DOM + ("feat",))
    placed = (
        P(DOM, "feat"),
        P("feat"),
        P(DOM, None, None),
        P(DOM),
        P(DOM, None, None),
        P("feat", None),
        P("feat"),
        P(DOM, "feat"),
    )
    return jax.shard_map(
        shards,
        mesh=fine,
        in_specs=placed,
        out_specs=(P(DOM, "feat"), P(None, "feat"), P("feat")),
        check_vma=False,
    )
```

```python
import functools
import math

import jax
import jax.numpy as jnp
from jax import lax
from jax.experimental import pallas as pl
from jax.experimental.pallas import tpu as pltpu
from jax.sharding import Mesh, PartitionSpec as P

DOM = ("z_far", "z_near", "y", "core")
NEAR = ("z_near", "y", "core")
PLANE = ("y", "core")
RING = ("z_far", "z_near")
NT = (((1,), (1,)), ((), ()))
LOW = 256
CODE = 128
ORDER = (2, 1, 3)
F32 = jnp.float32
BF16 = jnp.bfloat16


def as_column(row):
    size = row.shape[1]
    same = lax.broadcasted_iota(jnp.int32, (size, size), 0) == lax.broadcasted_iota(jnp.int32, (size, size), 1)
    return jnp.sum(jnp.where(same, row, 0.0), axis=1, keepdims=True)


def keep_kernel(keep_ref, features_ref, lists_ref, *refs):
    out_refs, code_ref = refs[:-1], refs[-1]
    planes = len(out_refs)
    rows, block = out_refs[0].shape
    kept = keep_ref.shape[1]
    nodes = features_ref.shape[1]
    lists = lists_ref.shape[0] // planes
    lane = lax.broadcasted_iota(jnp.int32, (kept, features_ref.shape[0]), 1)
    wanted = as_column(keep_ref[...].astype(F32)).astype(jnp.int32)
    select = jnp.where(lane == wanted, 1.0, 0.0).astype(BF16)
    columns = jnp.dot(select, features_ref[...], preferred_element_type=F32).astype(BF16)
    row = lists_ref[...]
    code = lax.shift_left(CODE + (row & (CODE - 1)), row // CODE)
    code_ref[...] = (code.astype(F32) * (1.0 / CODE)).astype(BF16)
    me = lax.axis_index("z_far")
    for ahead, out_ref in enumerate(out_refs):
        for tile in range(nodes // block):
            out_ref[tile * kept : (tile + 1) * kept, :] = columns[:, tile * block : (tile + 1) * block]
        first = pl.multiple_of(lax.bitwise_xor(me, ahead) * lists, lists)
        out_ref[rows - lists :, :] = code_ref[pl.ds(first, lists), :]


def keep(keep_cols, features, lists, planes):
    peers, block = lists.shape
    nodes = features.shape[1]
    kept = keep_cols.shape[0]
    rows = nodes // block * kept + peers // planes
    vmem = pl.BlockSpec(memory_space=pltpu.VMEM)
    return pl.pallas_call(
        keep_kernel,
        in_specs=[vmem] * 3,
        out_specs=[vmem] * planes,
        out_shape=[jax.ShapeDtypeStruct((rows, block), BF16)] * planes,
        scratch_shapes=[pltpu.VMEM(lists.shape, BF16)],
        name="keep_columns",
    )(keep_cols[None, :], features, lists)


def pick_kernel(held_ref, *rest):
    out_ref = rest[-1]
    lists, _, kept, block = out_ref.shape
    tiles = (held_ref.shape[0] - lists) // kept
    span = LOW // block
    highs = tiles // span
    table = jnp.concatenate(
        [
            jnp.concatenate([held_ref[t * kept : (t + 1) * kept, :] for t in range(h * span, (h + 1) * span)], axis=1)
            for h in range(highs)
        ],
        axis=0,
    )
    code = (held_ref[tiles * kept :, :].astype(F32) * CODE).astype(jnp.int32)
    shift = jnp.zeros((lists, block), jnp.int32)
    for step in range(1, tiles + 1):
        shift += jnp.where(code >= CODE << step, 1, 0)
    row = shift * CODE + (lax.shift_right_logical(code, shift) - CODE)
    sub = lax.broadcasted_iota(jnp.int32, (LOW, 2 * block), 0).astype(F32).astype(BF16)
    for pair in range(lists // 2):
        rows = jnp.concatenate([row[2 * pair : 2 * pair + 1, :], row[2 * pair + 1 : 2 * pair + 2, :]], axis=1)
        low = (rows & (LOW - 1)).astype(F32).astype(BF16)
        high = rows // LOW
        onehot = jnp.where(sub == low, jnp.ones((), BF16), jnp.zeros((), BF16))
        found = jnp.dot(table, onehot, preferred_element_type=F32)
        total = jnp.zeros((kept, 2 * block), F32)
        for step in range(highs):
            total = jnp.where(high == step, found[step * kept : (step + 1) * kept], total)
        total = total.astype(BF16)
        out_ref[2 * pair, 0] = total[:, :block]
        out_ref[2 * pair + 1, 0] = total[:, block:]


def pick(held, part, parts, lists, kept, before):
    rows, block = held.shape
    earlier = [] if before is None else [before]
    return pl.pallas_call(
        pick_kernel,
        grid=(1,),
        in_specs=[pl.BlockSpec((rows, block), lambda i: (0, 0))]
        + [pl.BlockSpec(memory_space=pl.ANY)] * len(earlier),
        out_specs=pl.BlockSpec((lists, 1, kept, block), lambda i: (0, part, 0, 0)),
        out_shape=jax.ShapeDtypeStruct((lists, parts, kept, block), BF16),
        input_output_aliases={1: 0} if earlier else {},
        compiler_params=pltpu.CompilerParams(vmem_limit_bytes=24 << 20),
        cost_estimate=pl.CostEstimate(
            flops=2 * lists * block * LOW * block, bytes_accessed=2 * block * (lists * kept + rows), transcendentals=0
        ),
        name="pick_rows",
    )(held, *earlier)


def aggregate_kernel(tiles_row, cols_ref, own_ref, incoming_ref, vals_ref, out_ref):
    kept, block = incoming_ref.shape[1:]
    own = vals_ref.shape[0] // tiles_row
    for tile in range(vals_ref.shape[0] // tiles_row):
        values, picked = [], []
        for term in range(tiles_row):
            at = tile * tiles_row + term
            column = cols_ref[at]
            mine = own_ref[pl.ds(pl.multiple_of(jnp.minimum(column, own - 1) * kept, kept), kept), :]
            theirs = incoming_ref[jnp.maximum(column - own, 0)]
            picked.append(jnp.where(column < own, mine, theirs))
            values.append(vals_ref[at])
        total = lax.dot_general(
            jnp.concatenate(picked, axis=1), jnp.concatenate(values, axis=1), NT, preferred_element_type=F32
        )
        for copy in range(out_ref.shape[0]):
            out_ref[copy, :, tile * block : (tile + 1) * block] = total


def aggregate(tile_cols, own, incoming, tile_vals, copies):
    kept, block = incoming.shape[1:]
    tiles = own.shape[0] // kept
    vmem = pl.BlockSpec(memory_space=pltpu.VMEM)
    return pl.pallas_call(
        functools.partial(aggregate_kernel, tile_cols.shape[0] // tiles),
        in_specs=[pl.BlockSpec(memory_space=pltpu.SMEM), vmem, vmem, vmem],
        out_specs=vmem,
        out_shape=jax.ShapeDtypeStruct((copies, kept, tiles * block), F32),
        compiler_params=pltpu.CompilerParams(vmem_limit_bytes=24 << 20),
        name="aggregate_tiles",
    )(tile_cols, own, incoming, tile_vals)


def layer_kernel(agg_ref, weight_ref, grad_ref, out_ref, terms_ref):
    hidden, nodes = grad_ref.shape
    step = 256
    depth = agg_ref.shape[0]
    slope = math.sqrt(2.0 / math.pi)
    weight = jnp.concatenate([weight_ref[:, :depth].astype(BF16)] * 3, axis=1)
    bias = jnp.concatenate([weight_ref[:, depth:]] * (step // depth), axis=1)
    grad_weight = jnp.zeros((hidden, depth), F32)
    grad_bias = jnp.zeros((hidden, 1), F32)
    for start in range(0, nodes, step):
        exact = agg_ref[:, start : start + step]
        first = exact.astype(BF16)
        rest = exact - first.astype(F32)
        second = rest.astype(BF16)
        third = (rest - second.astype(F32)).astype(BF16)
        pre = jnp.dot(weight, jnp.concatenate([first, second, third], axis=0), preferred_element_type=F32)
        pre = pre + bias
        square = pre * pre
        bend = jnp.tanh(slope * (pre + 0.044715 * (pre * square)))
        half = 0.5 * (1.0 + bend)
        out_ref[:, start : start + step] = (pre * half).astype(BF16)
        inner = slope * (1.0 + 3 * 0.044715 * square)
        pull = half + 0.5 * pre * ((1.0 - bend) * (1.0 + bend)) * inner
        grad_pre = grad_ref[:, start : start + step].astype(F32) * pull
        grad_bias += jnp.sum(grad_pre, axis=1, keepdims=True)
        upper = grad_pre.astype(BF16)
        lower = (grad_pre - upper.astype(F32)).astype(BF16)
        both = lax.dot_general(
            jnp.concatenate([upper, lower], axis=0),
            jnp.concatenate([first, second], axis=0),
            NT,
            preferred_element_type=F32,
        )
        grad_weight += (both[:hidden, depth:] + both[hidden:, :depth]) + both[:hidden, :depth]
    groups = terms_ref.shape[0]
    rows = hidden // groups
    lane = lax.broadcasted_iota(jnp.int32, (hidden, depth), 1)
    spot = lax.broadcasted_iota(jnp.int32, (hidden, depth), 0)
    diagonal = jnp.where(lane == spot, grad_bias, 0.0).reshape(groups, rows, depth)
    terms_ref[:, :rows, :] = grad_weight.reshape(groups, rows, depth)
    terms_ref[:, rows:, :] = jnp.broadcast_to(jnp.sum(diagonal, axis=1, keepdims=True), (groups, rows, depth))


def layer(aggregated, weight, grad_out, groups):
    depth, nodes = aggregated.shape
    hidden = weight.shape[0]
    vmem = pl.BlockSpec(memory_space=pltpu.VMEM)
    return pl.pallas_call(
        layer_kernel,
        in_specs=[vmem] * 3,
        out_specs=[vmem] * 2,
        out_shape=[
            jax.ShapeDtypeStruct((hidden, nodes), BF16),
            jax.ShapeDtypeStruct((groups, 2 * hidden // groups, depth), F32),
        ],
        compiler_params=pltpu.CompilerParams(vmem_limit_bytes=24 << 20),
        name="layer_and_gradient",
    )(aggregated, weight, grad_out)


def unpack_kernel(terms_ref, weight_ref, bias_ref):
    groups = terms_ref.shape[0]
    hidden, depth = weight_ref.shape
    rows = hidden // groups
    weight_ref[...] = terms_ref[:, :rows, :].reshape(hidden, depth)
    bias_ref[...] = jnp.sum(terms_ref[:, rows : rows + 1, :], axis=0)[:, :hidden]


def unpack(terms, hidden):
    depth = terms.shape[2]
    vmem = pl.BlockSpec(memory_space=pltpu.VMEM)
    return pl.pallas_call(
        unpack_kernel,
        in_specs=[vmem],
        out_specs=[vmem] * 2,
        out_shape=[jax.ShapeDtypeStruct((hidden, depth), F32), jax.ShapeDtypeStruct((1, hidden), F32)],
        compiler_params=pltpu.CompilerParams(vmem_limit_bytes=24 << 20),
        name="unpack_gradients",
    )(terms)


def spread(array, axis):
    size = lax.axis_size(axis)
    return lax.all_to_all(jnp.broadcast_to(array[None], (size,) + array.shape), axis, 0, 0)


def shards(features, keep_cols, send_rows, tile_cols, tile_vals, weight, bias, grad_out):
    feat = lax.axis_size("feat")
    hidden = bias.shape[0]
    kept = keep_cols.shape[0]
    planes = lax.axis_size("z_far")
    near = lax.axis_size(NEAR)
    block = send_rows.shape[2]
    outgoing = keep(keep_cols, features.T, send_rows[0], planes)
    own = outgoing[0][: features.shape[0] // block * kept]
    held = [outgoing[0]] + [None] * (planes - 1)
    for ahead in ORDER:
        held[ahead] = lax.ppermute(outgoing[ahead], "z_far", [(i, i ^ ahead) for i in range(planes)])
    picked = None
    for ahead in (0,) + ORDER:
        picked = pick(held[ahead], ahead, planes, near, kept, picked)
    picked = picked.reshape(near, planes * kept, block)
    incoming = lax.all_to_all(picked, NEAR, 0, 0)
    incoming = incoming.reshape(near * planes, kept, block)
    tiles = features.shape[0] // block
    sender = tile_cols - tiles
    behind = lax.bitwise_xor(lax.axis_index("z_far"), lax.div(sender, near))
    place = tiles + lax.rem(sender, near) * planes + behind
    tile_cols = jnp.where(sender < 0, tile_cols, place)
    weight_all = lax.all_gather(weight, "feat", axis=0, tiled=True)
    columns = lax.dynamic_slice_in_dim(weight_all, lax.axis_index("feat") * hidden, hidden, 1).T
    bias = jnp.broadcast_to(bias[:, None], columns.shape)
    columns = jnp.concatenate([columns.astype(F32), bias], axis=1)
    incoming, columns, tile_cols = lax.optimization_barrier((incoming, columns, tile_cols))
    aggregated = aggregate(tile_cols, own, incoming, tile_vals, feat)
    aggregated = lax.all_to_all(aggregated, "feat", 0, 0).reshape(feat * kept, -1)
    groups = lax.axis_size(PLANE)
    out, terms = layer(aggregated, columns, grad_out.T, groups)
    terms = lax.all_to_all(terms, PLANE, 0, 0).sum(axis=0)
    rows = hidden // groups + 1
    packed = spread(terms[:rows].reshape(1, -1), RING).sum(axis=0).reshape(rows, -1)
    terms = spread(jnp.pad(packed, ((0, terms.shape[0] - rows), (0, 0))), PLANE)
    grad_weight, grad_bias = unpack(terms, hidden)
    return out.T, grad_weight.T, grad_bias.reshape(hidden)


def solution(mesh):
    devices = mesh.devices.reshape(4, 4, 4, 2, mesh.shape["feat"])
    fine = Mesh(devices, DOM + ("feat",))
    placed = (
        P(DOM, "feat"),
        P("feat"),
        P(DOM, None, None),
        P(DOM),
        P(DOM, None, None),
        P("feat", None),
        P("feat"),
        P(DOM, "feat"),
    )
    return jax.shard_map(
        shards,
        mesh=fine,
        in_specs=placed,
        out_specs=(P(DOM, "feat"), P(None, "feat"), P("feat")),
        check_vma=False,
    )
```

```python
import functools
import math

import jax
import jax.numpy as jnp
from jax import lax
from jax.experimental import pallas as pl
from jax.experimental.pallas import tpu as pltpu
from jax.sharding import Mesh, PartitionSpec as P

DOM = ("z_far", "z_near", "y", "core")
NEAR = ("z_near", "y", "core")
PLANE = ("y", "core")
RING = ("z_far", "z_near")
NT = (((1,), (1,)), ((), ()))
LOW = 256
CODE = 128
ORDER = (2, 1, 3)
F32 = jnp.float32
BF16 = jnp.bfloat16


def as_column(row):
    size = row.shape[1]
    same = lax.broadcasted_iota(jnp.int32, (size, size), 0) == lax.broadcasted_iota(jnp.int32, (size, size), 1)
    return jnp.sum(jnp.where(same, row, 0.0), axis=1, keepdims=True)


def keep_kernel(planes, *refs):
    sources, out_refs = refs[:3], refs[3 : 3 + planes]
    keep_ref, features_ref, lists_ref, kept_ref, code_ref, read_sems, write_sems = refs[3 + planes :]
    reads = [
        pltpu.make_async_copy(source, target, read_sems.at[place])
        for place, (source, target) in enumerate(zip(sources, (keep_ref, features_ref, lists_ref)))
    ]
    for read in reads[::-1]:
        read.start()
    kept = keep_ref.shape[1]
    block = lists_ref.shape[1]
    nodes = features_ref.shape[1]
    lists = lists_ref.shape[0] // planes
    rows = kept_ref.shape[0]
    writes = []
    reads[2].wait()
    row = lists_ref[...]
    code = lax.shift_left(CODE + (row & (CODE - 1)), row // CODE)
    code_ref[...] = (code.astype(F32) * (1.0 / CODE)).astype(BF16)
    me = lax.axis_index("z_far")
    for ahead, out_ref in enumerate(out_refs):
        first = pl.multiple_of(lax.rem(me + ahead, planes) * lists, lists)
        source = code_ref.at[pl.ds(first, lists), :]
        writes.append(pltpu.make_async_copy(source, out_ref.at[pl.ds(rows, lists), :], write_sems.at[2 * ahead]))
        writes[-1].start()
    reads[0].wait()
    lane = lax.broadcasted_iota(jnp.int32, (kept, features_ref.shape[0]), 1)
    wanted = as_column(keep_ref[...].astype(F32)).astype(jnp.int32)
    select = jnp.where(lane == wanted, 1.0, 0.0).astype(BF16)
    reads[1].wait()
    columns = jnp.dot(select, features_ref[...], preferred_element_type=F32).astype(BF16)
    for tile in range(nodes // block):
        kept_ref[tile * kept : (tile + 1) * kept, :] = columns[:, tile * block : (tile + 1) * block]
    for ahead, out_ref in enumerate(out_refs):
        writes.append(pltpu.make_async_copy(kept_ref, out_ref.at[pl.ds(0, rows), :], write_sems.at[2 * ahead + 1]))
        writes[-1].start()
    for write in writes:
        write.wait()


def keep(keep_cols, features, lists, planes):
    peers, block = lists.shape
    kept = keep_cols.shape[0]
    rows = features.shape[1] // block * kept
    hbm = pl.BlockSpec(memory_space=pl.ANY)
    return pl.pallas_call(
        functools.partial(keep_kernel, planes),
        in_specs=[hbm] * 3,
        out_specs=[hbm] * planes,
        out_shape=[jax.ShapeDtypeStruct((rows + peers // planes, block), BF16)] * planes,
        scratch_shapes=[
            pltpu.VMEM((1, kept), jnp.int32),
            pltpu.VMEM(features.shape, BF16),
            pltpu.VMEM(lists.shape, jnp.int32),
            pltpu.VMEM((rows, block), BF16),
            pltpu.VMEM(lists.shape, BF16),
            pltpu.SemaphoreType.DMA((3,)),
            pltpu.SemaphoreType.DMA((2 * planes,)),
        ],
        name="keep_columns",
    )(keep_cols[None, :], features, lists)


def pick_kernel(held_ref, *rest):
    out_ref = rest[-1]
    lists, _, kept, block = out_ref.shape
    tiles = (held_ref.shape[0] - lists) // kept
    span = LOW // block
    highs = tiles // span
    table = jnp.concatenate(
        [
            jnp.concatenate([held_ref[t * kept : (t + 1) * kept, :] for t in range(h * span, (h + 1) * span)], axis=1)
            for h in range(highs)
        ],
        axis=0,
    )
    code = (held_ref[tiles * kept :, :].astype(F32) * CODE).astype(jnp.int32)
    shift = jnp.zeros((lists, block), jnp.int32)
    for step in range(1, tiles + 1):
        shift += jnp.where(code >= CODE << step, 1, 0)
    row = shift * CODE + (lax.shift_right_logical(code, shift) - CODE)
    sub = lax.broadcasted_iota(jnp.int32, (LOW, 2 * block), 0).astype(F32).astype(BF16)
    for pair in range(lists // 2):
        rows = jnp.concatenate([row[2 * pair : 2 * pair + 1, :], row[2 * pair + 1 : 2 * pair + 2, :]], axis=1)
        low = (rows & (LOW - 1)).astype(F32).astype(BF16)
        high = rows // LOW
        onehot = jnp.where(sub == low, jnp.ones((), BF16), jnp.zeros((), BF16))
        found = jnp.dot(table, onehot, preferred_element_type=F32)
        total = jnp.zeros((kept, 2 * block), F32)
        for step in range(highs):
            total = jnp.where(high == step, found[step * kept : (step + 1) * kept], total)
        total = total.astype(BF16)
        out_ref[2 * pair, 0] = total[:, :block]
        out_ref[2 * pair + 1, 0] = total[:, block:]


def pick(held, part, parts, lists, kept, before):
    rows, block = held.shape
    earlier = [] if before is None else [before]
    return pl.pallas_call(
        pick_kernel,
        grid=(1,),
        in_specs=[pl.BlockSpec((rows, block), lambda i: (0, 0))]
        + [pl.BlockSpec(memory_space=pl.ANY)] * len(earlier),
        out_specs=pl.BlockSpec((lists, 1, kept, block), lambda i: (0, part, 0, 0)),
        out_shape=jax.ShapeDtypeStruct((lists, parts, kept, block), BF16),
        input_output_aliases={1: 0} if earlier else {},
        compiler_params=pltpu.CompilerParams(vmem_limit_bytes=24 << 20),
        cost_estimate=pl.CostEstimate(
            flops=2 * lists * block * LOW * block, bytes_accessed=2 * block * (lists * kept + rows), transcendentals=0
        ),
        name="pick_rows",
    )(held, *earlier)


def aggregate_kernel(tiles_row, cols_ref, own_ref, incoming_ref, vals_ref, out_ref):
    kept, block = incoming_ref.shape[1:]
    own = vals_ref.shape[0] // tiles_row
    for tile in range(vals_ref.shape[0] // tiles_row):
        values, picked = [], []
        for term in range(tiles_row):
            at = tile * tiles_row + term
            column = cols_ref[at]
            mine = own_ref[pl.ds(pl.multiple_of(jnp.minimum(column, own - 1) * kept, kept), kept), :]
            theirs = incoming_ref[jnp.maximum(column - own, 0)]
            picked.append(jnp.where(column < own, mine, theirs))
            values.append(vals_ref[at])
        total = lax.dot_general(
            jnp.concatenate(picked, axis=1), jnp.concatenate(values, axis=1), NT, preferred_element_type=F32
        )
        for copy in range(out_ref.shape[0]):
            out_ref[copy, :, tile * block : (tile + 1) * block] = total


def aggregate(tile_cols, own, incoming, tile_vals, copies):
    kept, block = incoming.shape[1:]
    tiles = own.shape[0] // kept
    vmem = pl.BlockSpec(memory_space=pltpu.VMEM)
    return pl.pallas_call(
        functools.partial(aggregate_kernel, tile_cols.shape[0] // tiles),
        in_specs=[pl.BlockSpec(memory_space=pltpu.SMEM), vmem, vmem, vmem],
        out_specs=vmem,
        out_shape=jax.ShapeDtypeStruct((copies, kept, tiles * block), F32),
        compiler_params=pltpu.CompilerParams(vmem_limit_bytes=24 << 20),
        name="aggregate_tiles",
    )(tile_cols, own, incoming, tile_vals)


def layer_kernel(agg_ref, weight_ref, grad_ref, out_ref, terms_ref):
    hidden, nodes = grad_ref.shape
    step = 256
    depth = agg_ref.shape[0]
    slope = math.sqrt(2.0 / math.pi)
    weight = jnp.concatenate([weight_ref[:, :depth].astype(BF16)] * 3, axis=1)
    bias = jnp.concatenate([weight_ref[:, depth:]] * (step // depth), axis=1)
    grad_weight = jnp.zeros((hidden, depth), F32)
    grad_bias = jnp.zeros((hidden, 1), F32)
    for start in range(0, nodes, step):
        exact = agg_ref[:, start : start + step]
        first = exact.astype(BF16)
        rest = exact - first.astype(F32)
        second = rest.astype(BF16)
        third = (rest - second.astype(F32)).astype(BF16)
        pre = jnp.dot(weight, jnp.concatenate([first, second, third], axis=0), preferred_element_type=F32)
        pre = pre + bias
        square = pre * pre
        bend = jnp.tanh(slope * (pre + 0.044715 * (pre * square)))
        half = 0.5 * (1.0 + bend)
        out_ref[:, start : start + step] = (pre * half).astype(BF16)
        inner = slope * (1.0 + 3 * 0.044715 * square)
        pull = half + 0.5 * pre * ((1.0 - bend) * (1.0 + bend)) * inner
        grad_pre = grad_ref[:, start : start + step].astype(F32) * pull
        grad_bias += jnp.sum(grad_pre, axis=1, keepdims=True)
        upper = grad_pre.astype(BF16)
        lower = (grad_pre - upper.astype(F32)).astype(BF16)
        both = lax.dot_general(
            jnp.concatenate([upper, lower], axis=0),
            jnp.concatenate([first, second], axis=0),
            NT,
            preferred_element_type=F32,
        )
        grad_weight += (both[:hidden, depth:] + both[hidden:, :depth]) + both[:hidden, :depth]
    groups = terms_ref.shape[0]
    rows = hidden // groups
    lane = lax.broadcasted_iota(jnp.int32, (hidden, depth), 1)
    spot = lax.broadcasted_iota(jnp.int32, (hidden, depth), 0)
    diagonal = jnp.where(lane == spot, grad_bias, 0.0).reshape(groups, rows, depth)
    terms_ref[:, :rows, :] = grad_weight.reshape(groups, rows, depth)
    terms_ref[:, rows:, :] = jnp.broadcast_to(jnp.sum(diagonal, axis=1, keepdims=True), (groups, rows, depth))


def layer(aggregated, weight, grad_out, groups):
    depth, nodes = aggregated.shape
    hidden = weight.shape[0]
    vmem = pl.BlockSpec(memory_space=pltpu.VMEM)
    return pl.pallas_call(
        layer_kernel,
        in_specs=[vmem] * 3,
        out_specs=[vmem] * 2,
        out_shape=[
            jax.ShapeDtypeStruct((hidden, nodes), BF16),
            jax.ShapeDtypeStruct((groups, 2 * hidden // groups, depth), F32),
        ],
        compiler_params=pltpu.CompilerParams(vmem_limit_bytes=24 << 20),
        name="layer_and_gradient",
    )(aggregated, weight, grad_out)


def unpack_kernel(terms_ref, weight_ref, bias_ref):
    groups = terms_ref.shape[0]
    hidden, depth = weight_ref.shape
    rows = hidden // groups
    weight_ref[...] = terms_ref[:, :rows, :].reshape(hidden, depth)
    bias_ref[...] = jnp.sum(terms_ref[:, rows : rows + 1, :], axis=0)[:, :hidden]


def unpack(terms, hidden):
    depth = terms.shape[2]
    vmem = pl.BlockSpec(memory_space=pltpu.VMEM)
    return pl.pallas_call(
        unpack_kernel,
        in_specs=[vmem],
        out_specs=[vmem] * 2,
        out_shape=[jax.ShapeDtypeStruct((hidden, depth), F32), jax.ShapeDtypeStruct((1, hidden), F32)],
        compiler_params=pltpu.CompilerParams(vmem_limit_bytes=24 << 20),
        name="unpack_gradients",
    )(terms)


def spread(array, axis):
    size = lax.axis_size(axis)
    return lax.all_to_all(jnp.broadcast_to(array[None], (size,) + array.shape), axis, 0, 0)


def shards(features, keep_cols, send_rows, tile_cols, tile_vals, weight, bias, grad_out):
    feat = lax.axis_size("feat")
    hidden = bias.shape[0]
    kept = keep_cols.shape[0]
    planes = lax.axis_size("z_far")
    near = lax.axis_size(NEAR)
    block = send_rows.shape[2]
    outgoing = keep(keep_cols, features.T, send_rows[0], planes)
    own = outgoing[0][: features.shape[0] // block * kept]
    held = [outgoing[0]] + [None] * (planes - 1)
    for ahead in ORDER:
        held[ahead] = lax.ppermute(outgoing[ahead], "z_far", [(i, (i + ahead) % planes) for i in range(planes)])
    picked = None
    for ahead in (0,) + ORDER:
        picked = pick(held[ahead], ahead, planes, near, kept, picked)
    picked = picked.reshape(near, planes * kept, block)
    incoming = lax.all_to_all(picked, NEAR, 0, 0)
    incoming = incoming.reshape(near * planes, kept, block)
    tiles = features.shape[0] // block
    sender = tile_cols - tiles
    behind = lax.rem(lax.axis_index("z_far") + planes - lax.div(sender, near), planes)
    place = tiles + lax.rem(sender, near) * planes + behind
    tile_cols = jnp.where(sender < 0, tile_cols, place)
    weight_all = lax.all_gather(weight, "feat", axis=0, tiled=True)
    columns = lax.dynamic_slice_in_dim(weight_all, lax.axis_index("feat") * hidden, hidden, 1).T
    bias = jnp.broadcast_to(bias[:, None], columns.shape)
    columns = jnp.concatenate([columns.astype(F32), bias], axis=1)
    incoming, columns, tile_cols = lax.optimization_barrier((incoming, columns, tile_cols))
    aggregated = aggregate(tile_cols, own, incoming, tile_vals, feat)
    aggregated = lax.all_to_all(aggregated, "feat", 0, 0).reshape(feat * kept, -1)
    groups = lax.axis_size(PLANE)
    out, terms = layer(aggregated, columns, grad_out.T, groups)
    terms = lax.all_to_all(terms, PLANE, 0, 0).sum(axis=0)
    rows = hidden // groups + 1
    packed = spread(terms[:rows].reshape(1, -1), RING).sum(axis=0).reshape(rows, -1)
    terms = spread(jnp.pad(packed, ((0, terms.shape[0] - rows), (0, 0))), PLANE)
    grad_weight, grad_bias = unpack(terms, hidden)
    return out.T, grad_weight.T, grad_bias.reshape(hidden)


def solution(mesh):
    devices = mesh.devices.reshape(4, 4, 4, 2, mesh.shape["feat"])
    fine = Mesh(devices, DOM + ("feat",))
    placed = (
        P(DOM, "feat"),
        P("feat"),
        P(DOM, None, None),
        P(DOM),
        P(DOM, None, None),
        P("feat", None),
        P("feat"),
        P(DOM, "feat"),
    )
    return jax.shard_map(
        shards,
        mesh=fine,
        in_specs=placed,
        out_specs=(P(DOM, "feat"), P(None, "feat"), P("feat")),
        check_vma=False,
    )
```
